32 devices in a mesh: seq: 2 (over y), head: 4 (over x, core), ctx: 4 (over z).
Axes of the slice: x: 2, y: 2, z: 4, core: 2. Of those that a mesh axis runs over, the one named last changes fastest.
Arguments:
- q_new: bfloat16 [1024, 8192], P('seq', ('head', 'ctx')), may hold values from -6 to 6
- k_prefix: bfloat16 [1024, 1024], P('seq', 'head'), may hold values from -204 to 204
- v_prefix: bfloat16 [1024, 1024], P('seq', 'head'), may hold values from -6 to 6
- k_new: bfloat16 [1024, 1024], P('seq', 'head'), may hold values from -204 to 204
- v_new: bfloat16 [1024, 1024], P('seq', 'head'), may hold values from -6 to 6
- block_offsets: int32 [8], P('seq'), may hold values from 0 to 511
- dec_hidden: bfloat16 [256, 8192], P(None, 'ctx'), may hold values from -6 to 6
- w_query: bfloat16 [8192, 4, 2048], P('ctx', 'head', 'seq'), may hold values from -0.0625 to 0.0625
- w_out: bfloat16 [4, 2048, 8192], P('head', 'seq', 'ctx'), may hold values from -0.0625 to 0.0625
- k_own: bfloat16 [256, 1024], P(None, 'head'), may hold values from -21 to 21
- v_own: bfloat16 [256, 1024], P(None, 'head'), may hold values from -6 to 6
- valid_len: int32 [256], replicated, may hold values from 1 to 1024
- parent: int32 [256], replicated, may hold values from 0 to 1023
Outputs:
- prefill_out: bfloat16 [1024, 8192], P('seq', ('head', 'ctx'))
- decoded: bfloat16 [256, 8192], P(('seq', 'head'), 'ctx')
The draws below stay inside these ranges and needn't reach their ends.
All inputs are finite; a program needn't handle non-finite values.
Results may differ from the reference program's by a relative error of at most 0.017.
The reference program's roundings to bfloat16 on the way count: a program that leaves them out, or rounds other values in their place, can miss the bound.
Values may be sent and summed in bfloat16 or wider, within the bound.
A program may use at most 64 MiB of HBM per device.

```python
import math
import jax
import jax.numpy as jnp
from jax import lax

D = 8192
HQ = 64
KVH = 8
HD = 128
ROWS = 256
QBLK = 128
PREFIX = 1024
NEW = 1024
GROUPS = 4


def spiky_keys(key, count, salt):
    base_key = jax.random.fold_in(key, 11 + salt)
    base = jax.random.truncated_normal(base_key, -6.0, 6.0, (count, KVH * HD), jnp.float32)
    return base.astype(jnp.bfloat16)


def draw_k_prefix(key, part):
    return spiky_keys(key, PREFIX, 0)


def draw_k_new(key, part):
    return spiky_keys(key, NEW, 101)


def plant(entries, stream_key, least, largest):
    shape = entries.shape
    index_at = [jax.random.randint(jax.random.fold_in(stream_key, axis), (), 0, shape[axis]) for axis in range(len(shape))]
    entries = entries.at[tuple(index_at)].set(least)
    longest = shape.index(max(shape))
    index_at[longest] = (index_at[longest] + 1) % shape[longest]
    return entries.at[tuple(index_at)].set(largest)


def level_of(own_key, extent, cuts, low, high):
    def one(axis_at, blocks):
        draws = jax.random.uniform(jax.random.fold_in(jax.random.fold_in(own_key, 6), axis_at), (blocks,), jnp.float32, low / len(cuts), high / len(cuts))
        return jnp.repeat(jnp.exp(draws), extent[axis_at] // blocks).reshape((-1,) + (1,) * (len(extent) - axis_at - 1))

    loudness = one(*cuts[0])
    for cut in cuts[1:]:
        loudness = loudness * one(*cut)
    return loudness


def scatter_about(stream_key, dims, scale, reach, split=(), kind=jnp.bfloat16):
    loudness = level_of(stream_key, dims, split, -0.22, 0.18) if split else 1.0
    result = jax.random.normal(stream_key, dims, jnp.float32) * scale * loudness
    return jnp.minimum(jnp.maximum(result, -reach), reach).astype(kind)


def setup_inputs(seed: int = 0) -> dict:
    streams_of = jax.random.split(jax.random.key(seed), 14)
    return {
        "q_new": scatter_about(streams_of[0], (NEW, HQ * HD), 1.0, 6.0, ((0, 2), (1, 16))),
        "k_prefix": draw_k_prefix(jax.random.fold_in(streams_of[13], 71), 0),
        "v_prefix": scatter_about(streams_of[2], (PREFIX, KVH * HD), 1.0, 6.0, ((0, 2), (1, 4))),
        "k_new": draw_k_new(jax.random.fold_in(streams_of[13], 71), 0),
        "v_new": scatter_about(streams_of[4], (NEW, KVH * HD), 1.0, 6.0, ((0, 2), (1, 4))),
        "block_offsets": plant(jax.random.randint(streams_of[5], (NEW // QBLK,), 0, PREFIX // 2), jax.random.fold_in(streams_of[5], 1), 0, (PREFIX // 2) - 1).astype(jnp.int32),
        "dec_hidden": scatter_about(streams_of[6], (ROWS, D), 1.0, 6.0, ((1, 4),)),
        "w_query": scatter_about(streams_of[7], (D, GROUPS, HQ // GROUPS * HD), D ** -0.5, 0.0625, ((0, 4), (1, 4), (2, 2))),
        "w_out": scatter_about(streams_of[8], (GROUPS, HQ // GROUPS * HD, D), D ** -0.5, 0.0625, ((0, 4), (1, 2), (2, 4))),
        "k_own": scatter_about(streams_of[9], (ROWS, KVH * HD), 3.5, 21.0, ((1, 4),)),
        "v_own": scatter_about(streams_of[10], (ROWS, KVH * HD), 1.0, 6.0, ((1, 4),)),
        "valid_len": plant(jax.random.randint(streams_of[11], (ROWS,), 1, PREFIX + 1), jax.random.fold_in(streams_of[11], 1), 1, PREFIX).astype(jnp.int32),
        "parent": plant(jax.random.randint(streams_of[12], (ROWS,), 0, NEW), jax.random.fold_in(streams_of[12], 1), 0, NEW - 1).astype(jnp.int32),
    }


def reference(q_new, k_prefix, v_prefix, k_new, v_new, block_offsets, dec_hidden, w_query, w_out, k_own, v_own, valid_len, parent):
    group_size = HQ // KVH
    scale = 1.0 / math.sqrt(HD)
    total_len = PREFIX + NEW
    keys = jnp.concatenate([k_prefix, k_new], axis=0).astype(jnp.float32).reshape(total_len, KVH, HD)
    values = jnp.concatenate([v_prefix, v_new], axis=0).astype(jnp.float32).reshape(total_len, KVH, HD)
    positions = jnp.arange(total_len, dtype=jnp.int32)
    firsts = jnp.repeat(block_offsets, QBLK)

    def prefill_block(inputs):
        query_blk, index_blk, first_blk = inputs
        queries = query_blk.astype(jnp.float32).reshape(QBLK, KVH, group_size, HD)
        scores = jnp.einsum('qkgd,tkd->qkgt', queries, keys) * scale
        visible = (positions[None, :] < PREFIX) & (positions[None, :] >= first_blk[:, None]) | (positions[None, :] >= PREFIX) & (positions[None, :] - PREFIX <= index_blk[:, None])
        scores = jnp.where(visible[:, None, None, :], scores, -jnp.inf)
        top = lax.optimization_barrier(jnp.max(scores, axis=-1, keepdims=True))
        weights = jnp.exp(scores - top)
        denom = lax.optimization_barrier(jnp.sum(weights, axis=-1))
        rounded = lax.optimization_barrier(weights.astype(jnp.bfloat16)).astype(jnp.float32)
        out = jnp.einsum('qkgt,tkd->qkgd', rounded, values) / denom[..., None]
        return out.astype(jnp.bfloat16).reshape(QBLK, HQ * HD)
    nblk = NEW // QBLK
    prefill_out = lax.map(prefill_block, (q_new.reshape(nblk, QBLK, HQ * HD), jnp.arange(NEW, dtype=jnp.int32).reshape(nblk, QBLK), firsts.reshape(nblk, QBLK))).reshape(NEW, HQ * HD)
    queries_all = jnp.dot(dec_hidden, w_query.reshape(D, HQ * HD), preferred_element_type=jnp.float32).astype(jnp.bfloat16)
    row_blk = math.gcd(ROWS, 32)
    rblocks = ROWS // row_blk

    def decode_block(inputs):
        query_blk, own_k, own_v, length_blk, parent_blk = inputs
        queries = query_blk.astype(jnp.float32).reshape(row_blk, KVH, group_size, HD)
        ownk = own_k.astype(jnp.float32).reshape(row_blk, KVH, HD)
        ownv = own_v.astype(jnp.float32).reshape(row_blk, KVH, HD)
        scores = jnp.einsum('rkgd,tkd->rkgt', queries, keys) * scale
        visible = (positions[None, :] < PREFIX) & (positions[None, :] < length_blk[:, None]) | (positions[None, :] >= PREFIX) & (positions[None, :] - PREFIX <= parent_blk[:, None])
        scores = jnp.where(visible[:, None, None, :], scores, -jnp.inf)
        own_score = jnp.einsum('rkgd,rkd->rkg', queries, ownk) * scale
        top = jnp.maximum(lax.optimization_barrier(jnp.max(scores, axis=-1)), own_score)
        weights = jnp.exp(scores - top[..., None])
        own_w = jnp.exp(own_score - top)
        denom = lax.optimization_barrier(jnp.sum(weights, axis=-1)) + own_w
        rounded = lax.optimization_barrier(weights.astype(jnp.bfloat16)).astype(jnp.float32)
        own_r = lax.optimization_barrier(own_w.astype(jnp.bfloat16)).astype(jnp.float32)
        out = jnp.einsum('rkgt,tkd->rkgd', rounded, values) + own_r[..., None] * ownv[:, :, None, :]
        out = out / denom[..., None]
        return out.astype(jnp.bfloat16).reshape(row_blk, HQ * HD)
    attn = lax.map(decode_block, (queries_all.reshape(rblocks, row_blk, HQ * HD), k_own.reshape(rblocks, row_blk, KVH * HD), v_own.reshape(rblocks, row_blk, KVH * HD), valid_len.reshape(rblocks, row_blk), parent.reshape(rblocks, row_blk))).reshape(ROWS, HQ * HD)
    decoded = jnp.dot(attn, w_out.reshape(HQ * HD, D), preferred_element_type=jnp.float32).astype(jnp.bfloat16)
    return (prefill_out, decoded)
```

```python
import functools
import math

import jax
import jax.numpy as jnp
from jax import lax
from jax.experimental import pallas as pl
from jax.experimental.pallas import tpu as pltpu
from jax.sharding import PartitionSpec as P

HQ = 64
KVH = 8
HD = 128
QBLK = 128
GROUP = HQ // KVH
NEG = -1e30
MESH = pl.DeviceIdType.MESH
F32 = jnp.float32
BF16 = jnp.bfloat16
C2 = math.log2(math.e) / math.sqrt(HD)


def dot_t(a, b):
    return lax.dot_general(a, b, (((1,), (1,)), ((), ())), preferred_element_type=F32)


def absorb(state, queries, keys, values, visible):
    best, total, accum = state
    scores = jnp.where(visible, dot_t(queries, keys) * C2, NEG)
    fresh = jnp.maximum(best, jnp.max(scores, axis=1, keepdims=True))
    factor = jnp.exp2(best - fresh)
    weights = jnp.exp2(scores - fresh)
    total = total * factor + jnp.sum(weights, axis=1, keepdims=True)
    accum = accum * factor + jnp.dot(weights.astype(BF16), values, preferred_element_type=F32)
    return fresh, total, accum


def kernel(
    sizes,
    q_hbm, kp_hbm, vp_hbm, kn_hbm, vn_hbm, off_ref, x_hbm, wq_hbm, wo_hbm, ko_ref, vo_ref, lim_ref,
    pre_ref, dec_ref,
    q, kv, x, wq, wo, qpart, qrecv, attn, opart, orecv, m_s, l_s, a_s,
    load_sem, wq_sem, wo_sem, kv_load, kv_send, kv_recv, q_send, q_recv, a_send, a_recv, o_send, o_recv,
):
    n_seq, n_head, n_ctx, q_chunk, o_chunk = sizes
    seq, head, ctx = lax.axis_index("seq"), lax.axis_index("head"), lax.axis_index("ctx")
    block, width = q.shape
    per_dev = width // HD
    n_blk = block // QBLK
    n_out = n_seq * n_head
    me_out = seq * n_head + head
    rows, cols_q = x.shape[0], wq.shape[1]
    r_ctx, r_out = rows // n_ctx, rows // n_out
    heads_dec = cols_q // HD
    n_qc, n_oc = cols_q // q_chunk, wo.shape[1] // o_chunk

    load_x = pltpu.make_async_copy(x_hbm, x, load_sem.at[0])
    load_x.start()
    load_wq = []
    for c in range(n_qc):
        part = pl.ds(c * q_chunk, q_chunk)
        load_wq.append(pltpu.make_async_copy(wq_hbm.at[:, part], wq.at[:, part], wq_sem.at[c]))
        load_wq[-1].start()
    sources = (kp_hbm, vp_hbm, kn_hbm, vn_hbm)
    load_kv = [pltpu.make_async_copy(s, kv.at[0, i], kv_load.at[i]) for i, s in enumerate(sources)]
    load_q = pltpu.make_async_copy(q_hbm, q, load_sem.at[1])
    for c in load_kv + [load_q]:
        c.start()
    load_wo = pltpu.make_async_copy(wo_hbm, wo, wo_sem)
    load_wo.start()

    def out_peer(d):
        t = lax.rem(me_out + d, n_out)
        return {"seq": t // n_head, "head": lax.rem(t, n_head)}

    barrier = pltpu.get_barrier_semaphore()
    for d in range(1, n_ctx):
        pl.semaphore_signal(
            barrier, inc=1, device_id={"ctx": lax.rem(ctx + d, n_ctx)}, device_id_type=MESH
        )
    for d in range(1, n_out):
        pl.semaphore_signal(barrier, inc=1, device_id=out_peer(d), device_id_type=MESH)
    pl.semaphore_wait(barrier, n_ctx - 1 + n_out - 1)

    def remote(src, dst, send, recv, to):
        copy = pltpu.make_async_remote_copy(
            src_ref=src, dst_ref=dst, send_sem=send, recv_sem=recv, device_id=to, device_id_type=MESH
        )
        copy.start()
        return copy

    sent = []
    kv_copies = []
    for d in range(1, n_seq):
        to = {"seq": lax.rem(seq + d, n_seq)}
        for i, s in enumerate(sources):
            kv_copies.append(remote(s, kv.at[d, i], kv_send.at[d, i], kv_recv.at[d, i], to))

    load_x.wait()
    q_copies = []
    for c in range(n_qc):
        load_wq[c].wait()
        part = slice(c * q_chunk, (c + 1) * q_chunk)
        prod = jnp.dot(x[...], wq[:, part], preferred_element_type=F32)
        for i in range(n_ctx):
            qpart[c, i] = prod[i * r_ctx:(i + 1) * r_ctx]
        for d in range(1, n_ctx):
            to = lax.rem(ctx + d, n_ctx)
            q_copies.append(
                remote(qpart.at[c, to], qrecv.at[c, d], q_send.at[c, d], q_recv.at[c, d], {"ctx": to})
            )

    def stacked(b):
        tokens = pl.ds(pl.multiple_of(b * QBLK, QBLK), QBLK)
        return jnp.concatenate([q[tokens, h * HD:(h + 1) * HD] for h in range(per_dev)], axis=0)

    lanes_pre = pl.ds(pl.multiple_of(ctx * per_dev // GROUP * HD, HD), HD)
    token = lax.broadcasted_iota(jnp.int32, (QBLK, block), 0)
    key = lax.broadcasted_iota(jnp.int32, (QBLK, block), 1)

    def tile(a, n):
        return jnp.concatenate([a] * n, axis=0) if n > 1 else a

    def prefill_step(state, queries, b, d):
        base = lax.rem(seq - d + n_seq, n_seq) * block
        seen = key + base <= token + (seq * block + b * QBLK)
        state = absorb(
            state, queries, kv[d, 2, :, lanes_pre], kv[d, 3, :, lanes_pre], tile(seen, per_dev)
        )
        seen = key + base >= off_ref[b]
        return absorb(
            state, queries, kv[d, 0, :, lanes_pre], kv[d, 1, :, lanes_pre], tile(seen, per_dev)
        )

    for c in load_kv + [load_q]:
        c.wait()
    rp = per_dev * QBLK

    def local_block(b, _):
        zero = jnp.zeros((rp, 1), F32)
        m, l, a = prefill_step((zero + NEG, zero, jnp.zeros((rp, HD), F32)), stacked(b), b, 0)
        m_s[b], l_s[b], a_s[b] = m, l, a
        return 0

    lax.fori_loop(0, n_blk, local_block, 0)

    for c in kv_copies:
        c.wait_recv()
    for c in q_copies:
        c.wait_recv()
    parts = []
    for c in range(n_qc):
        total = qpart[c, ctx]
        for d in range(1, n_ctx):
            total = total + qrecv[c, d]
        total = total.astype(BF16)
        parts += [total[:, h * HD:(h + 1) * HD] for h in range(q_chunk // HD)]
    dq = jnp.concatenate(parts, axis=0)
    lanes_dec = pl.ds(pl.multiple_of(seq * heads_dec // GROUP * HD, HD), HD)
    mine = pl.ds(pl.multiple_of(ctx * r_ctx, r_ctx), r_ctx)
    own_k = tile(ko_ref[mine, lanes_dec].astype(F32), heads_dec)
    own_v = tile(vo_ref[mine, lanes_dec].astype(F32), heads_dec)
    limits = lim_ref[mine, :]
    length, parent = limits[:, 0:1], limits[:, 1:2]
    own = jnp.sum(dq.astype(F32) * own_k, axis=1, keepdims=True) * C2
    dkey = lax.broadcasted_iota(jnp.int32, (r_ctx, block), 1)

    def decode_step(d, state):
        pos = dkey + lax.rem(seq - d + n_seq, n_seq) * block
        state = absorb(
            state, dq, kv[d, 0, :, lanes_dec], kv[d, 1, :, lanes_dec], tile(pos < length, heads_dec)
        )
        return absorb(
            state, dq, kv[d, 2, :, lanes_dec], kv[d, 3, :, lanes_dec], tile(pos <= parent, heads_dec)
        )

    _, total, accum = lax.fori_loop(0, n_seq, decode_step, (own, jnp.ones_like(own), own_v))
    result = (accum / total).astype(BF16)
    for h in range(heads_dec):
        attn[0, :, h * HD:(h + 1) * HD] = result[h * r_ctx:(h + 1) * r_ctx]
    a_copies = [
        remote(attn.at[0], attn.at[d], a_send.at[d], a_recv.at[d], {"ctx": lax.rem(ctx + d, n_ctx)})
        for d in range(1, n_ctx)
    ]

    def remote_block(b, _):
        queries = stacked(b)
        state = lax.fori_loop(
            1, n_seq, lambda d, st: prefill_step(st, queries, b, d), (m_s[b], l_s[b], a_s[b])
        )
        out = (state[2] / state[1]).astype(BF16)
        tokens = pl.ds(pl.multiple_of(b * QBLK, QBLK), QBLK)
        for h in range(per_dev):
            pre_ref[tokens, h * HD:(h + 1) * HD] = out[h * QBLK:(h + 1) * QBLK]
        return 0

    lax.fori_loop(0, n_blk, remote_block, 0)

    load_wo.wait()
    for c in a_copies:
        c.wait_recv()
    full = jnp.concatenate([attn[lax.rem(ctx - i + n_ctx, n_ctx)] for i in range(n_ctx)], axis=0)
    o_copies = []
    for c in range(n_oc):
        prod = jnp.dot(full, wo[:, c * o_chunk:(c + 1) * o_chunk], preferred_element_type=F32)
        for i in range(n_out):
            opart[c, i] = prod[i * r_out:(i + 1) * r_out].astype(BF16)
        for d in range(1, n_out):
            to = lax.rem(me_out + d, n_out)
            o_copies.append(
                remote(opart.at[c, to], orecv.at[c, d], o_send.at[c, d], o_recv.at[c, d], out_peer(d))
            )
    for c in range(n_oc):
        acc = opart[c, me_out].astype(F32)
        for d in range(1, n_out):
            o_copies[c * (n_out - 1) + d - 1].wait_recv()
            acc = acc + orecv[c, d].astype(F32)
        dec_ref[:, c * o_chunk:(c + 1) * o_chunk] = acc.astype(BF16)
    for c in kv_copies + q_copies + a_copies + o_copies:
        c.wait_send()


def body(
    q_new, k_prefix, v_prefix, k_new, v_new, block_offsets, dec_hidden, w_query, w_out, k_own, v_own,
    valid_len, parent,
):
    n_seq, n_head, n_ctx = (lax.axis_size(a) for a in ("seq", "head", "ctx"))
    n_out = n_seq * n_head
    block, width = q_new.shape
    rows = dec_hidden.shape[0]
    wq = w_query.reshape(w_query.shape[0], -1)
    wo = w_out.reshape(-1, w_out.shape[2])
    q_chunk = math.gcd(wq.shape[1], 512)
    o_chunk = math.gcd(wo.shape[1], 512)
    n_qc, n_oc = wq.shape[1] // q_chunk, wo.shape[1] // o_chunk
    limits = jnp.stack([valid_len, parent], axis=1)
    n_blk, rp = block // QBLK, width // HD * QBLK
    hbm, vmem = pl.BlockSpec(memory_space=pl.ANY), pl.BlockSpec(memory_space=pltpu.VMEM)
    smem = pl.BlockSpec(memory_space=pltpu.SMEM)
    dma = pltpu.SemaphoreType.DMA
    r_ctx, r_out = rows // n_ctx, rows // n_out
    return pl.pallas_call(
        functools.partial(kernel, (n_seq, n_head, n_ctx, q_chunk, o_chunk)),
        out_shape=(
            jax.ShapeDtypeStruct(q_new.shape, BF16),
            jax.ShapeDtypeStruct((r_out, wo.shape[1]), BF16),
        ),
        in_specs=[hbm] * 5 + [smem] + [hbm] * 3 + [vmem] * 3,
        out_specs=(vmem, vmem),
        scratch_shapes=[
            pltpu.VMEM(q_new.shape, BF16),
            pltpu.VMEM((n_seq, 4) + k_new.shape, BF16),
            pltpu.VMEM(dec_hidden.shape, BF16),
            pltpu.VMEM(wq.shape, BF16),
            pltpu.VMEM(wo.shape, BF16),
            pltpu.VMEM((n_qc, n_ctx, r_ctx, q_chunk), F32),
            pltpu.VMEM((n_qc, n_ctx, r_ctx, q_chunk), F32),
            pltpu.VMEM((n_ctx, r_ctx, wo.shape[0]), BF16),
            pltpu.VMEM((n_oc, n_out, r_out, o_chunk), BF16),
            pltpu.VMEM((n_oc, n_out, r_out, o_chunk), BF16),
            pltpu.VMEM((n_blk, rp, 1), F32),
            pltpu.VMEM((n_blk, rp, 1), F32),
            pltpu.VMEM((n_blk, rp, HD), F32),
            dma((2,)), dma((n_qc,)), dma, dma((4,)),
            dma((n_seq, 4)), dma((n_seq, 4)),
            dma((n_qc, n_ctx)), dma((n_qc, n_ctx)),
            dma((n_ctx,)), dma((n_ctx,)),
            dma((n_oc, n_out)), dma((n_oc, n_out)),
        ],
        compiler_params=pltpu.CompilerParams(
            collective_id=0, has_side_effects=True, vmem_limit_bytes=56 * 1024 * 1024
        ),
    )(q_new, k_prefix, v_prefix, k_new, v_new, block_offsets, dec_hidden, wq, wo, k_own, v_own, limits)


def solution(mesh):
    in_specs = (
        P("seq", ("head", "ctx")),
        P("seq", "head"),
        P("seq", "head"),
        P("seq", "head"),
        P("seq", "head"),
        P("seq"),
        P(None, "ctx"),
        P("ctx", "head", "seq"),
        P("head", "seq", "ctx"),
        P(None, "head"),
        P(None, "head"),
        P(),
        P(),
    )
    out_specs = (P("seq", ("head", "ctx")), P(("seq", "head"), "ctx"))
    return jax.shard_map(body, mesh=mesh, in_specs=in_specs, out_specs=out_specs, check_vma=False)
```

```python
import functools
import math

import jax
import jax.numpy as jnp
from jax import lax
from jax.experimental import pallas as pl
from jax.experimental.pallas import tpu as pltpu
from jax.sharding import PartitionSpec as P

HQ = 64
KVH = 8
HD = 128
QBLK = 128
GROUP = HQ // KVH
NEG = -1e30
MESH = pl.DeviceIdType.MESH
F32 = jnp.float32
BF16 = jnp.bfloat16
C2 = math.log2(math.e) / math.sqrt(HD)


def dot_t(a, b):
    return lax.dot_general(a, b, (((1,), (1,)), ((), ())), preferred_element_type=F32)


def absorb(state, queries, keys, values, visible):
    best, total, accum = state
    scores = jnp.where(visible, dot_t(queries, keys) * C2, NEG)
    fresh = jnp.maximum(best, jnp.max(scores, axis=1, keepdims=True))
    factor = jnp.exp2(best - fresh)
    weights = jnp.exp2(scores - fresh)
    total = total * factor + jnp.sum(weights, axis=1, keepdims=True)
    accum = accum * factor + jnp.dot(weights.astype(BF16), values, preferred_element_type=F32)
    return fresh, total, accum


def kernel(
    sizes,
    q_hbm, kp_hbm, vp_hbm, kn_hbm, vn_hbm, off_ref, x_hbm, wq_hbm, wo_hbm, ko_ref, vo_ref, len_ref, par_ref,
    pre_ref, dec_ref,
    q, kv, x, wq, wo, qpart, qrecv, attn, opart, pair, osum, orecv, m_s, l_s, a_s,
    load_sem, wq_sem, wo_sem, kv_load, kv_send, kv_recv, q_send, q_recv, a_send, a_recv, p_send, p_recv, o_send, o_recv,
):
    n_seq, n_head, n_ctx, q_chunk, o_chunk = sizes
    seq, head, ctx = lax.axis_index("seq"), lax.axis_index("head"), lax.axis_index("ctx")
    block, width = q.shape
    per_dev = width // HD
    n_blk = block // QBLK
    n_kvh = kv.shape[3] // HD
    n_out = n_seq * n_head
    me_out = seq * n_head + head
    rows, cols_q = x.shape[0], wq.shape[1]
    r_ctx, r_out = rows // n_ctx, rows // n_out
    heads_dec = cols_q // HD
    n_qc, n_oc = cols_q // q_chunk, wo.shape[1] // o_chunk

    load_x = pltpu.make_async_copy(x_hbm, x, load_sem.at[0])
    load_x.start()
    load_wq = []
    for c in range(n_qc):
        part = pl.ds(c * q_chunk, q_chunk)
        load_wq.append(pltpu.make_async_copy(wq_hbm.at[:, part], wq.at[:, part], wq_sem.at[c]))
        load_wq[-1].start()
    sources = (kp_hbm, vp_hbm, kn_hbm, vn_hbm)
    load_kv = [pltpu.make_async_copy(s, kv.at[0, i], kv_load.at[i]) for i, s in enumerate(sources)]
    load_q = pltpu.make_async_copy(q_hbm, q, load_sem.at[1])
    for c in load_kv + [load_q]:
        c.start()
    load_wo = pltpu.make_async_copy(wo_hbm, wo, wo_sem)
    load_wo.start()

    def out_peer(d):
        t = lax.rem(me_out + d, n_out)
        return {"seq": t // n_head, "head": lax.rem(t, n_head)}

    barrier = pltpu.get_barrier_semaphore()
    for d in range(1, n_ctx):
        pl.semaphore_signal(
            barrier, inc=1, device_id={"ctx": lax.rem(ctx + d, n_ctx)}, device_id_type=MESH
        )
    for d in range(1, n_out):
        pl.semaphore_signal(barrier, inc=1, device_id=out_peer(d), device_id_type=MESH)
    pl.semaphore_wait(barrier, n_ctx - 1 + n_out - 1)

    def remote(src, dst, send, recv, to):
        copy = pltpu.make_async_remote_copy(
            src_ref=src, dst_ref=dst, send_sem=send, recv_sem=recv, device_id=to, device_id_type=MESH
        )
        copy.start()
        return copy

    kv_copies = [[] for _ in range(n_kvh)]
    for d in range(1, n_seq):
        to = {"seq": lax.rem(seq + d, n_seq)}
        first = to["seq"] * heads_dec // GROUP
        for j in range(n_kvh):
            lanes = pl.ds(pl.multiple_of(lax.rem(first + j, n_kvh) * HD, HD), HD)
            for i, s in enumerate(sources):
                kv_copies[j].append(
                    remote(
                        s.at[:, lanes], kv.at[d, i, :, lanes],
                        kv_send.at[d, i, j], kv_recv.at[d, i, j], to,
                    )
                )

    load_x.wait()
    q_copies = []
    for c in range(n_qc):
        load_wq[c].wait()
        part = slice(c * q_chunk, (c + 1) * q_chunk)
        prod = jnp.dot(x[...], wq[:, part], preferred_element_type=F32)
        for i in range(n_ctx):
            qpart[c, i] = prod[i * r_ctx:(i + 1) * r_ctx]
        for d in range(1, n_ctx):
            to = lax.rem(ctx + d, n_ctx)
            q_copies.append(
                remote(qpart.at[c, to], qrecv.at[c, d], q_send.at[c, d], q_recv.at[c, d], {"ctx": to})
            )

    def stacked(b):
        tokens = pl.ds(pl.multiple_of(b * QBLK, QBLK), QBLK)
        return jnp.concatenate([q[tokens, h * HD:(h + 1) * HD] for h in range(per_dev)], axis=0)

    lanes_pre = pl.ds(pl.multiple_of(ctx * per_dev // GROUP * HD, HD), HD)
    token = lax.broadcasted_iota(jnp.int32, (QBLK, block), 0)
    key = lax.broadcasted_iota(jnp.int32, (QBLK, block), 1)

    def tile(a, n):
        return jnp.concatenate([a] * n, axis=0) if n > 1 else a

    def prefill_step(state, queries, b, d):
        base = lax.rem(seq - d + n_seq, n_seq) * block
        seen = key + base <= token + (seq * block + b * QBLK)
        state = absorb(
            state, queries, kv[d, 2, :, lanes_pre], kv[d, 3, :, lanes_pre], tile(seen, per_dev)
        )
        seen = key + base >= off_ref[b]
        return absorb(
            state, queries, kv[d, 0, :, lanes_pre], kv[d, 1, :, lanes_pre], tile(seen, per_dev)
        )

    for c in load_kv + [load_q]:
        c.wait()
    rp = per_dev * QBLK

    def local_block(b, _):
        zero = jnp.zeros((rp, 1), F32)
        m, l, a = prefill_step((zero + NEG, zero, jnp.zeros((rp, HD), F32)), stacked(b), b, 0)
        m_s[b], l_s[b], a_s[b] = m, l, a
        return 0

    lax.fori_loop(0, n_blk, local_block, 0)

    lanes_dec = pl.ds(pl.multiple_of(seq * heads_dec // GROUP * HD, HD), HD)
    mine = pl.ds(pl.multiple_of(ctx * r_ctx, r_ctx), r_ctx)
    h_chunk = q_chunk // HD
    own_k = tile(ko_ref[mine, lanes_dec].astype(F32), h_chunk)
    own_v = tile(vo_ref[mine, lanes_dec].astype(F32), h_chunk)
    row_at = lax.broadcasted_iota(jnp.int32, (r_ctx, rows), 0) + ctx * r_ctx
    diagonal = row_at == lax.broadcasted_iota(jnp.int32, (r_ctx, rows), 1)
    length = jnp.sum(jnp.where(diagonal, len_ref[...], 0), axis=1, keepdims=True)
    parent = jnp.sum(jnp.where(diagonal, par_ref[...], 0), axis=1, keepdims=True)
    dkey = lax.broadcasted_iota(jnp.int32, (r_ctx, block), 1)

    def decode_step(d, state, dq):
        pos = dkey + lax.rem(seq - d + n_seq, n_seq) * block
        state = absorb(
            state, dq, kv[d, 0, :, lanes_dec], kv[d, 1, :, lanes_dec], tile(pos < length, h_chunk)
        )
        return absorb(
            state, dq, kv[d, 2, :, lanes_dec], kv[d, 3, :, lanes_dec], tile(pos <= parent, h_chunk)
        )

    for c in kv_copies[0]:
        c.wait_recv()
    a_copies = []
    for c in range(n_qc):
        for d in range(1, n_ctx):
            q_copies[c * (n_ctx - 1) + d - 1].wait_recv()
        total = qpart[c, ctx]
        for d in range(1, n_ctx):
            total = total + qrecv[c, d]
        total = total.astype(BF16)
        dq = jnp.concatenate([total[:, h * HD:(h + 1) * HD] for h in range(h_chunk)], axis=0)
        own = jnp.sum(dq.astype(F32) * own_k, axis=1, keepdims=True) * C2
        _, total, accum = lax.fori_loop(
            0, n_seq, lambda d, state: decode_step(d, state, dq), (own, jnp.ones_like(own), own_v)
        )
        result = (accum / total).astype(BF16)
        for h in range(h_chunk):
            attn[c, 0, :, h * HD:(h + 1) * HD] = result[h * r_ctx:(h + 1) * r_ctx]
        for d in range(1, n_ctx):
            a_copies.append(
                remote(
                    attn.at[c, 0], attn.at[c, d], a_send.at[c, d], a_recv.at[c, d],
                    {"ctx": lax.rem(ctx + d, n_ctx)},
                )
            )

    def remote_block(b, _):
        queries = stacked(b)
        state = lax.fori_loop(
            1, n_seq, lambda d, st: prefill_step(st, queries, b, d), (m_s[b], l_s[b], a_s[b])
        )
        out = (state[2] / state[1]).astype(BF16)
        tokens = pl.ds(pl.multiple_of(b * QBLK, QBLK), QBLK)
        for h in range(per_dev):
            pre_ref[tokens, h * HD:(h + 1) * HD] = out[h * QBLK:(h + 1) * QBLK]
        return 0

    load_wo.wait()
    for c in a_copies:
        c.wait_recv()
    full = jnp.concatenate(
        [
            jnp.concatenate(
                [attn[c, lax.rem(ctx - i + n_ctx, n_ctx)] for i in range(n_ctx)], axis=0
            )
            for c in range(n_qc)
        ],
        axis=1,
    )
    core = lax.rem(head, 2)
    other = {"head": head + 1 - 2 * core}
    p_copies, o_copies = [], []
    for c in range(n_oc):
        prod = jnp.dot(full, wo[:, c * o_chunk:(c + 1) * o_chunk], preferred_element_type=F32)
        for i in range(n_out):
            opart[c, i % 2, i // 2] = prod[i * r_out:(i + 1) * r_out].astype(BF16)
        p_copies.append(
            remote(opart.at[c, 1 - core], pair.at[c], p_send.at[c], p_recv.at[c], other)
        )
    for c in range(n_oc):
        p_copies[c].wait_recv()
        for i in range(n_out // 2):
            osum[c, i] = (opart[c, core, i].astype(F32) + pair[c, i].astype(F32)).astype(BF16)
        for d in range(1, n_out // 2):
            t = lax.rem(me_out // 2 + d, n_out // 2)
            to = {"seq": t // (n_head // 2), "head": lax.rem(t, n_head // 2) * 2 + core}
            o_copies.append(
                remote(osum.at[c, t], orecv.at[c, d], o_send.at[c, d], o_recv.at[c, d], to)
            )
    for group in kv_copies[1:]:
        for c in group:
            c.wait_recv()
    lax.fori_loop(0, n_blk, remote_block, 0)
    for c in range(n_oc):
        acc = osum[c, me_out // 2].astype(F32)
        for d in range(1, n_out // 2):
            o_copies[c * (n_out // 2 - 1) + d - 1].wait_recv()
            acc = acc + orecv[c, d].astype(F32)
        dec_ref[:, c * o_chunk:(c + 1) * o_chunk] = acc.astype(BF16)
    for c in sum(kv_copies, []) + q_copies + a_copies + p_copies + o_copies:
        c.wait_send()


def body(
    q_new, k_prefix, v_prefix, k_new, v_new, block_offsets, dec_hidden, w_query, w_out, k_own, v_own,
    valid_len, parent,
):
    n_seq, n_head, n_ctx = (lax.axis_size(a) for a in ("seq", "head", "ctx"))
    n_out = n_seq * n_head
    block, width = q_new.shape
    rows = dec_hidden.shape[0]
    wq = w_query.reshape(w_query.shape[0], -1)
    wo = w_out.reshape(-1, w_out.shape[2])
    q_chunk = math.gcd(wq.shape[1], 512)
    o_chunk = math.gcd(wo.shape[1], 512)
    n_qc, n_oc = wq.shape[1] // q_chunk, wo.shape[1] // o_chunk
    n_kvh = k_new.shape[1] // HD
    n_blk, rp = block // QBLK, width // HD * QBLK
    hbm, vmem = pl.BlockSpec(memory_space=pl.ANY), pl.BlockSpec(memory_space=pltpu.VMEM)
    smem = pl.BlockSpec(memory_space=pltpu.SMEM)
    dma = pltpu.SemaphoreType.DMA
    r_ctx, r_out = rows // n_ctx, rows // n_out
    return pl.pallas_call(
        functools.partial(kernel, (n_seq, n_head, n_ctx, q_chunk, o_chunk)),
        out_shape=(
            jax.ShapeDtypeStruct(q_new.shape, BF16),
            jax.ShapeDtypeStruct((r_out, wo.shape[1]), BF16),
        ),
        in_specs=[hbm] * 5 + [smem] + [hbm] * 3 + [vmem] * 4,
        out_specs=(vmem, vmem),
        scratch_shapes=[
            pltpu.VMEM(q_new.shape, BF16),
            pltpu.VMEM((n_seq, 4) + k_new.shape, BF16),
            pltpu.VMEM(dec_hidden.shape, BF16),
            pltpu.VMEM(wq.shape, BF16),
            pltpu.VMEM(wo.shape, BF16),
            pltpu.VMEM((n_qc, n_ctx, r_ctx, q_chunk), F32),
            pltpu.VMEM((n_qc, n_ctx, r_ctx, q_chunk), F32),
            pltpu.VMEM((n_qc, n_ctx, r_ctx, q_chunk), BF16),
            pltpu.VMEM((n_oc, 2, n_out // 2, r_out, o_chunk), BF16),
            pltpu.VMEM((n_oc, n_out // 2, r_out, o_chunk), BF16),
            pltpu.VMEM((n_oc, n_out // 2, r_out, o_chunk), BF16),
            pltpu.VMEM((n_oc, n_out // 2, r_out, o_chunk), BF16),
            pltpu.VMEM((n_blk, rp, 1), F32),
            pltpu.VMEM((n_blk, rp, 1), F32),
            pltpu.VMEM((n_blk, rp, HD), F32),
            dma((2,)), dma((n_qc,)), dma, dma((4,)),
            dma((n_seq, 4, n_kvh)), dma((n_seq, 4, n_kvh)),
            dma((n_qc, n_ctx)), dma((n_qc, n_ctx)),
            dma((n_qc, n_ctx)), dma((n_qc, n_ctx)),
            dma((n_oc,)), dma((n_oc,)),
            dma((n_oc, n_out // 2)), dma((n_oc, n_out // 2)),
        ],
        compiler_params=pltpu.CompilerParams(
            collective_id=0, has_side_effects=True, vmem_limit_bytes=56 * 1024 * 1024
        ),
    )(q_new, k_prefix, v_prefix, k_new, v_new, block_offsets, dec_hidden, wq, wo, k_own, v_own, valid_len[None], parent[None])


def solution(mesh):
    in_specs = (
        P("seq", ("head", "ctx")),
        P("seq", "head"),
        P("seq", "head"),
        P("seq", "head"),
        P("seq", "head"),
        P("seq"),
        P(None, "ctx"),
        P("ctx", "head", "seq"),
        P("head", "seq", "ctx"),
        P(None, "head"),
        P(None, "head"),
        P(),
        P(),
    )
    out_specs = (P("seq", ("head", "ctx")), P(("seq", "head"), "ctx"))
    return jax.shard_map(body, mesh=mesh, in_specs=in_specs, out_specs=out_specs, check_vma=False)
```

```python
import functools
import math

import jax
import jax.numpy as jnp
from jax import lax
from jax.experimental import pallas as pl
from jax.experimental.pallas import tpu as pltpu
from jax.sharding import PartitionSpec as P

HQ = 64
KVH = 8
HD = 128
QBLK = 128
GROUP = HQ // KVH
NEG = -1e30
MESH = pl.DeviceIdType.MESH
F32 = jnp.float32
BF16 = jnp.bfloat16
C2 = math.log2(math.e) / math.sqrt(HD)


def dot_t(a, b):
    return lax.dot_general(a, b, (((1,), (1,)), ((), ())), preferred_element_type=F32)


def absorb(state, queries, keys, values, visible):
    best, total, accum = state
    scores = jnp.where(visible, dot_t(queries, keys) * C2, NEG)
    fresh = jnp.maximum(best, jnp.max(scores, axis=1, keepdims=True))
    factor = jnp.exp2(best - fresh)
    weights = jnp.exp2(scores - fresh)
    total = total * factor + jnp.sum(weights, axis=1, keepdims=True)
    accum = accum * factor + jnp.dot(weights.astype(BF16), values, preferred_element_type=F32)
    return fresh, total, accum


def kernel(
    sizes,
    q_hbm, kp_hbm, vp_hbm, kn_hbm, vn_hbm, off_ref, x_hbm, wq_hbm, wo_hbm, ko_ref, vo_ref, len_ref, par_ref,
    pre_ref, dec_ref,
    q, kv, x, wq, wo, qpart, qrecv, attn, opart, pair, osum, orecv, m_s, l_s, a_s,
    load_sem, wq_sem, wo_sem, kv_load, kv_send, kv_recv, q_send, q_recv, a_send, a_recv, p_send, p_recv, o_send, o_recv,
):
    n_seq, n_head, n_ctx, q_chunk, o_chunk = sizes
    seq, head, ctx = lax.axis_index("seq"), lax.axis_index("head"), lax.axis_index("ctx")
    block, width = q.shape
    per_dev = width // HD
    n_blk = block // QBLK
    n_kvh = kv.shape[3] // HD
    n_out = n_seq * n_head
    me_out = seq * n_head + head
    rows, cols_q = x.shape[0], wq.shape[1]
    r_ctx, r_out = rows // n_ctx, rows // n_out
    heads_dec = cols_q // HD
    n_qc, n_oc = cols_q // q_chunk, wo.shape[1] // o_chunk

    load_x = pltpu.make_async_copy(x_hbm, x, load_sem.at[0])
    load_x.start()
    load_wq = []
    for c in range(n_qc):
        part = pl.ds(c * q_chunk, q_chunk)
        load_wq.append(pltpu.make_async_copy(wq_hbm.at[:, part], wq.at[:, part], wq_sem.at[c]))
        load_wq[-1].start()
    sources = (kp_hbm, vp_hbm, kn_hbm, vn_hbm)
    load_kv = [pltpu.make_async_copy(s, kv.at[0, i], kv_load.at[i]) for i, s in enumerate(sources)]
    load_q = pltpu.make_async_copy(q_hbm, q, load_sem.at[1])
    for c in load_kv + [load_q]:
        c.start()
    load_wo = pltpu.make_async_copy(wo_hbm, wo, wo_sem)
    load_wo.start()

    def out_peer(d):
        t = lax.rem(me_out + d, n_out)
        return {"seq": t // n_head, "head": lax.rem(t, n_head)}

    barrier = pltpu.get_barrier_semaphore()
    for d in range(1, n_ctx):
        pl.semaphore_signal(
            barrier, inc=1, device_id={"ctx": lax.rem(ctx + d, n_ctx)}, device_id_type=MESH
        )
    for d in range(1, n_out):
        pl.semaphore_signal(barrier, inc=1, device_id=out_peer(d), device_id_type=MESH)
    pl.semaphore_wait(barrier, n_ctx - 1 + n_out - 1)

    def remote(src, dst, send, recv, to):
        copy = pltpu.make_async_remote_copy(
            src_ref=src, dst_ref=dst, send_sem=send, recv_sem=recv, device_id=to, device_id_type=MESH
        )
        copy.start()
        return copy

    kv_copies = [[] for _ in range(n_kvh)]
    for d in range(1, n_seq):
        to = {"seq": lax.rem(seq + d, n_seq)}
        first = to["seq"] * heads_dec // GROUP
        for j in range(n_kvh):
            lanes = pl.ds(pl.multiple_of(lax.rem(first + j, n_kvh) * HD, HD), HD)
            for i, s in enumerate(sources):
                kv_copies[j].append(
                    remote(
                        s.at[:, lanes], kv.at[d, i, :, lanes],
                        kv_send.at[d, i, j], kv_recv.at[d, i, j], to,
                    )
                )

    load_x.wait()
    q_copies = []
    for c in range(n_qc):
        load_wq[c].wait()
        part = slice(c * q_chunk, (c + 1) * q_chunk)
        prod = jnp.dot(x[...], wq[:, part], preferred_element_type=F32)
        for i in range(n_ctx):
            qpart[c, i] = prod[i * r_ctx:(i + 1) * r_ctx]
        for d in range(1, n_ctx):
            to = lax.rem(ctx + d, n_ctx)
            q_copies.append(
                remote(qpart.at[c, to], qrecv.at[c, d], q_send.at[c, d], q_recv.at[c, d], {"ctx": to})
            )

    def stacked(b):
        tokens = pl.ds(pl.multiple_of(b * QBLK, QBLK), QBLK)
        return jnp.concatenate([q[tokens, h * HD:(h + 1) * HD] for h in range(per_dev)], axis=0)

    lanes_pre = pl.ds(pl.multiple_of(ctx * per_dev // GROUP * HD, HD), HD)
    token = lax.broadcasted_iota(jnp.int32, (QBLK, block), 0)
    key = lax.broadcasted_iota(jnp.int32, (QBLK, block), 1)

    def tile(a, n):
        return jnp.concatenate([a] * n, axis=0) if n > 1 else a

    def prefill_step(state, queries, b, d):
        base = lax.rem(seq - d + n_seq, n_seq) * block
        seen = key + base <= token + (seq * block + b * QBLK)
        state = absorb(
            state, queries, kv[d, 2, :, lanes_pre], kv[d, 3, :, lanes_pre], tile(seen, per_dev)
        )
        seen = key + base >= off_ref[b]
        return absorb(
            state, queries, kv[d, 0, :, lanes_pre], kv[d, 1, :, lanes_pre], tile(seen, per_dev)
        )

    for c in load_kv + [load_q]:
        c.wait()
    rp = per_dev * QBLK

    def local_block(b, _):
        zero = jnp.zeros((rp, 1), F32)
        m, l, a = prefill_step((zero + NEG, zero, jnp.zeros((rp, HD), F32)), stacked(b), b, 0)
        m_s[b], l_s[b], a_s[b] = m, l, a
        return 0

    lax.fori_loop(0, n_blk, local_block, 0)

    lanes_dec = pl.ds(pl.multiple_of(seq * heads_dec // GROUP * HD, HD), HD)
    mine = pl.ds(pl.multiple_of(ctx * r_ctx, r_ctx), r_ctx)
    h_chunk = q_chunk // HD
    own_k = tile(ko_ref[mine, lanes_dec].astype(F32), h_chunk)
    own_v = tile(vo_ref[mine, lanes_dec].astype(F32), h_chunk)
    row_at = lax.broadcasted_iota(jnp.int32, (r_ctx, rows), 0) + ctx * r_ctx
    diagonal = row_at == lax.broadcasted_iota(jnp.int32, (r_ctx, rows), 1)
    length = jnp.sum(jnp.where(diagonal, len_ref[...], 0), axis=1, keepdims=True)
    parent = jnp.sum(jnp.where(diagonal, par_ref[...], 0), axis=1, keepdims=True)
    dkey = lax.broadcasted_iota(jnp.int32, (r_ctx, block), 1)

    def decode_step(d, state, dq):
        pos = dkey + lax.rem(seq - d + n_seq, n_seq) * block
        state = absorb(
            state, dq, kv[d, 0, :, lanes_dec], kv[d, 1, :, lanes_dec], tile(pos < length, h_chunk)
        )
        return absorb(
            state, dq, kv[d, 2, :, lanes_dec], kv[d, 3, :, lanes_dec], tile(pos <= parent, h_chunk)
        )

    def remote_block(b, _):
        queries = stacked(b)
        state = lax.fori_loop(
            1, n_seq, lambda d, st: prefill_step(st, queries, b, d), (m_s[b], l_s[b], a_s[b])
        )
        out = (state[2] / state[1]).astype(BF16)
        tokens = pl.ds(pl.multiple_of(b * QBLK, QBLK), QBLK)
        for h in range(per_dev):
            pre_ref[tokens, h * HD:(h + 1) * HD] = out[h * QBLK:(h + 1) * QBLK]
        return 0

    early = n_blk // 2 if n_qc > 1 else 0
    for c in kv_copies[0]:
        c.wait_recv()
    a_copies = []
    for c in range(n_qc):
        for d in range(1, n_ctx):
            q_copies[c * (n_ctx - 1) + d - 1].wait_recv()
        total = qpart[c, ctx]
        for d in range(1, n_ctx):
            total = total + qrecv[c, d]
        total = total.astype(BF16)
        dq = jnp.concatenate([total[:, h * HD:(h + 1) * HD] for h in range(h_chunk)], axis=0)
        own = jnp.sum(dq.astype(F32) * own_k, axis=1, keepdims=True) * C2
        _, total, accum = lax.fori_loop(
            0, n_seq, lambda d, state: decode_step(d, state, dq), (own, jnp.ones_like(own), own_v)
        )
        result = (accum / total).astype(BF16)
        for h in range(h_chunk):
            attn[c, 0, :, h * HD:(h + 1) * HD] = result[h * r_ctx:(h + 1) * r_ctx]
        for d in range(1, n_ctx):
            a_copies.append(
                remote(
                    attn.at[c, 0], attn.at[c, d], a_send.at[c, d], a_recv.at[c, d],
                    {"ctx": lax.rem(ctx + d, n_ctx)},
                )
            )
        if c == 0:
            for group in kv_copies[1:]:
                for copy in group:
                    copy.wait_recv()
            lax.fori_loop(0, early, remote_block, 0)

    load_wo.wait()
    for c in a_copies:
        c.wait_recv()
    full = jnp.concatenate(
        [
            jnp.concatenate(
                [attn[c, lax.rem(ctx - i + n_ctx, n_ctx)] for i in range(n_ctx)], axis=0
            )
            for c in range(n_qc)
        ],
        axis=1,
    )
    core = lax.rem(head, 2)
    other = {"head": head + 1 - 2 * core}
    p_copies, o_copies = [], []
    for c in range(n_oc):
        prod = jnp.dot(full, wo[:, c * o_chunk:(c + 1) * o_chunk], preferred_element_type=F32)
        for i in range(n_out):
            opart[c, i % 2, i // 2] = prod[i * r_out:(i + 1) * r_out].astype(BF16)
        p_copies.append(
            remote(opart.at[c, 1 - core], pair.at[c], p_send.at[c], p_recv.at[c], other)
        )
    for c in range(n_oc):
        p_copies[c].wait_recv()
        for i in range(n_out // 2):
            osum[c, i] = (opart[c, core, i].astype(F32) + pair[c, i].astype(F32)).astype(BF16)
        for d in range(1, n_out // 2):
            t = lax.rem(me_out // 2 + d, n_out // 2)
            to = {"seq": t // (n_head // 2), "head": lax.rem(t, n_head // 2) * 2 + core}
            o_copies.append(
                remote(osum.at[c, t], orecv.at[c, d], o_send.at[c, d], o_recv.at[c, d], to)
            )
    lax.fori_loop(early, n_blk, remote_block, 0)
    for c in range(n_oc):
        acc = osum[c, me_out // 2].astype(F32)
        for d in range(1, n_out // 2):
            o_copies[c * (n_out // 2 - 1) + d - 1].wait_recv()
            acc = acc + orecv[c, d].astype(F32)
        dec_ref[:, c * o_chunk:(c + 1) * o_chunk] = acc.astype(BF16)
    for c in sum(kv_copies, []) + q_copies + a_copies + p_copies + o_copies:
        c.wait_send()


def body(
    q_new, k_prefix, v_prefix, k_new, v_new, block_offsets, dec_hidden, w_query, w_out, k_own, v_own,
    valid_len, parent,
):
    n_seq, n_head, n_ctx = (lax.axis_size(a) for a in ("seq", "head", "ctx"))
    n_out = n_seq * n_head
    block, width = q_new.shape
    rows = dec_hidden.shape[0]
    wq = w_query.reshape(w_query.shape[0], -1)
    wo = w_out.reshape(-1, w_out.shape[2])
    q_chunk = math.gcd(wq.shape[1], 512)
    o_chunk = math.gcd(wo.shape[1], 512)
    n_qc, n_oc = wq.shape[1] // q_chunk, wo.shape[1] // o_chunk
    n_kvh = k_new.shape[1] // HD
    n_blk, rp = block // QBLK, width // HD * QBLK
    hbm, vmem = pl.BlockSpec(memory_space=pl.ANY), pl.BlockSpec(memory_space=pltpu.VMEM)
    smem = pl.BlockSpec(memory_space=pltpu.SMEM)
    dma = pltpu.SemaphoreType.DMA
    r_ctx, r_out = rows // n_ctx, rows // n_out
    return pl.pallas_call(
        functools.partial(kernel, (n_seq, n_head, n_ctx, q_chunk, o_chunk)),
        out_shape=(
            jax.ShapeDtypeStruct(q_new.shape, BF16),
            jax.ShapeDtypeStruct((r_out, wo.shape[1]), BF16),
        ),
        in_specs=[hbm] * 5 + [smem] + [hbm] * 3 + [vmem] * 4,
        out_specs=(vmem, vmem),
        scratch_shapes=[
            pltpu.VMEM(q_new.shape, BF16),
            pltpu.VMEM((n_seq, 4) + k_new.shape, BF16),
            pltpu.VMEM(dec_hidden.shape, BF16),
            pltpu.VMEM(wq.shape, BF16),
            pltpu.VMEM(wo.shape, BF16),
            pltpu.VMEM((n_qc, n_ctx, r_ctx, q_chunk), F32),
            pltpu.VMEM((n_qc, n_ctx, r_ctx, q_chunk), F32),
            pltpu.VMEM((n_qc, n_ctx, r_ctx, q_chunk), BF16),
            pltpu.VMEM((n_oc, 2, n_out // 2, r_out, o_chunk), BF16),
            pltpu.VMEM((n_oc, n_out // 2, r_out, o_chunk), BF16),
            pltpu.VMEM((n_oc, n_out // 2, r_out, o_chunk), BF16),
            pltpu.VMEM((n_oc, n_out // 2, r_out, o_chunk), BF16),
            pltpu.VMEM((n_blk, rp, 1), F32),
            pltpu.VMEM((n_blk, rp, 1), F32),
            pltpu.VMEM((n_blk, rp, HD), F32),
            dma((2,)), dma((n_qc,)), dma, dma((4,)),
            dma((n_seq, 4, n_kvh)), dma((n_seq, 4, n_kvh)),
            dma((n_qc, n_ctx)), dma((n_qc, n_ctx)),
            dma((n_qc, n_ctx)), dma((n_qc, n_ctx)),
            dma((n_oc,)), dma((n_oc,)),
            dma((n_oc, n_out // 2)), dma((n_oc, n_out // 2)),
        ],
        compiler_params=pltpu.CompilerParams(
            collective_id=0, has_side_effects=True, vmem_limit_bytes=56 * 1024 * 1024
        ),
    )(q_new, k_prefix, v_prefix, k_new, v_new, block_offsets, dec_hidden, wq, wo, k_own, v_own, valid_len[None], parent[None])


def solution(mesh):
    in_specs = (
        P("seq", ("head", "ctx")),
        P("seq", "head"),
        P("seq", "head"),
        P("seq", "head"),
        P("seq", "head"),
        P("seq"),
        P(None, "ctx"),
        P("ctx", "head", "seq"),
        P("head", "seq", "ctx"),
        P(None, "head"),
        P(None, "head"),
        P(),
        P(),
    )
    out_specs = (P("seq", ("head", "ctx")), P(("seq", "head"), "ctx"))
    return jax.shard_map(body, mesh=mesh, in_specs=in_specs, out_specs=out_specs, check_vma=False)
```
